32 devices in a mesh: groups: 2 (over y), ctx: 4 (over z), head: 2 (over x), sub: 2 (over core).
Axes of the slice: x: 2, y: 2, z: 4, core: 2. Of those that a mesh axis runs over, the one named last changes fastest.
Arguments:
- query_rows: bfloat16 [128, 128, 1024], P(('groups', 'ctx', 'sub'), 'head'), parts along dimension 0, may hold values from -16 to 16
- key_rows: bfloat16 [128, 128, 1024], P(('groups', 'ctx', 'sub'), 'head'), parts along dimension 0, may hold values from -6 to 6
- value_rows: bfloat16 [128, 128, 1024], P(('groups', 'ctx', 'sub'), 'head'), parts along dimension 0, may hold values from -4 to 4
- cotangent: bfloat16 [128, 128, 1024], P(('groups', 'ctx', 'sub'), 'head'), parts along dimension 0, may hold values from -4 to 4
- neighbours: int32 [128, 16], P('groups'), parts along dimension 0, may hold values from -1 to 63, as said below
- valid_counts: int32 [128], P('groups'), parts along dimension 0, may hold values from 32 to 128
Outputs:
- attended: bfloat16 [128, 128, 1024], P(('groups', 'ctx', 'sub'), 'head'), parts along dimension 0
- query_grad: bfloat16 [128, 128, 1024], P(('groups', 'ctx', 'sub'), 'head'), parts along dimension 0
- key_grad: bfloat16 [128, 128, 1024], P(('groups', 'ctx', 'sub'), 'head'), parts along dimension 0
- value_grad: bfloat16 [128, 128, 1024], P(('groups', 'ctx', 'sub'), 'head'), parts along dimension 0
The draws below stay inside these ranges and needn't reach their ends.
There are 2 independent parts, one for each index of `groups`. The reference program is written for one: setup_inputs(seed, part) draws one part's arguments, and reference() takes and returns one part's arrays. A program takes and returns all parts, laid end to end along the dimension named above; each array names one. Nothing has to cross between parts.
Inputs may be any that keep to these rules, and one draw needn't show every extreme that they name: `neighbours`: row b begins with b itself; its other entries are distinct blocks at most 8 blocks away from b, or -1 for an empty slot; a block with 8 blocks on both sides has no empty slot.
All inputs are finite; a program needn't handle non-finite values.
Results may differ from the reference program's by a relative error of at most 0.012.
Values may be sent and summed in bfloat16 or wider, within the bound.
A program may use at most 128 MiB of HBM per device.

```python
import jax
import jax.numpy as jnp
from jax import lax

DH = 128
BQ = 128
NBR = 16
WIN = 8
D = 1024
NBLK = 64


def paired_rows(key):
    base_key = jax.random.fold_in(key, 11)
    first_key, second_key = jax.random.split(base_key, 2)
    full_shape = (NBLK, BQ, D)
    query_draw = jnp.clip(jax.random.normal(first_key, full_shape, jnp.float32), -4.0, 4.0)
    keyset = jnp.clip(jax.random.normal(second_key, full_shape, jnp.float32), -4.0, 4.0)
    return (query_draw, keyset)


def draw_query_rows(key, part):
    return paired_rows(key)[0].astype(jnp.bfloat16)


def draw_key_rows(key, part):
    return paired_rows(key)[1].astype(jnp.bfloat16)


def draw_neighbours(key, part):
    blocks = jnp.arange(NBLK, dtype=jnp.int32)
    offsets = jnp.concatenate([jnp.arange(-WIN, 0, dtype=jnp.int32), jnp.arange(1, WIN + 1, dtype=jnp.int32)])
    candidate = blocks[:, None] + offsets[None, :]
    inside = (candidate >= 0) & (candidate < NBLK)
    noise = jax.random.randint(jax.random.fold_in(key, 5), (NBLK, 2 * WIN), 0, 1 << 20)
    column = jnp.arange(2 * WIN, dtype=jnp.int32)[None, :]
    ranking = jnp.where(inside, noise * 64 + column, -1 - column)
    unused, picked = lax.top_k(ranking, NBR - 1)
    chosen = jnp.take_along_axis(candidate, picked, axis=1)
    chosen_inside = jnp.take_along_axis(inside, picked, axis=1)
    chosen = jnp.where(chosen_inside, chosen, -1)
    return jnp.concatenate([blocks[:, None], chosen], axis=1).astype(jnp.int32)


def place_ends(values, stream_key, least, high):
    spot = [jax.random.randint(jax.random.fold_in(stream_key, axis), (), 0, length) for axis, length in enumerate(values.shape)]
    main_axis = values.shape.index(max(values.shape))
    next_to = spot[:main_axis] + [(spot[main_axis] + 1) % values.shape[main_axis]] + spot[main_axis + 1:]
    return values.at[tuple(spot)].set(least).at[tuple(next_to)].set(high)


def block_levels(stream_key, dims, shards, least, high):
    gain, own = 1.0, jax.random.fold_in(stream_key, 6)
    for dim, shards_of in shards:
        heights = jnp.exp(jax.random.uniform(jax.random.fold_in(own, dim), (shards_of,), jnp.float32, least / len(shards), high / len(shards)))
        gain = gain * jnp.repeat(heights, dims[dim] // shards_of).reshape([-1 if axis == dim else 1 for axis in range(len(dims))])
    return gain


def normal_values(key, shape, deviation, bound, shards=(), kind=jnp.bfloat16):
    values = deviation * jax.random.normal(key, shape, jnp.float32)
    if shards:
        values = values * block_levels(key, shape, shards, -0.22, 0.18)
    return jnp.clip(values, -bound, bound).astype(kind)


def setup_inputs(seed: int = 0, part: int = 0) -> dict:
    splits = jax.random.split(jax.random.key(seed), 7)
    part_keys = jax.random.split(jax.random.fold_in(splits[6], part), 7)
    query_rows = draw_query_rows(jax.random.fold_in(jax.random.fold_in(splits[6], part), 71), part)
    key_rows = draw_key_rows(jax.random.fold_in(jax.random.fold_in(splits[6], part), 71), part)
    value_rows = normal_values(part_keys[2], (NBLK, BQ, D), 1.0, 4.0, ((0, 8), (1, 2)))
    cotangent = normal_values(part_keys[3], (NBLK, BQ, D), 1.0, 4.0, ((0, 8), (1, 2)))
    neighbours = draw_neighbours(jax.random.fold_in(jax.random.fold_in(splits[6], part), 71), part)
    valid_counts = place_ends(jax.random.randint(part_keys[5], (NBLK,), BQ // 4, BQ + 1), jax.random.fold_in(part_keys[5], 1), BQ // 4, BQ).astype(jnp.int32)
    return dict(query_rows=query_rows, key_rows=key_rows, value_rows=value_rows, cotangent=cotangent, neighbours=neighbours, valid_counts=valid_counts)


NEGATIVE = -1.0e30


def split_heads(tile_rows):
    return tile_rows.reshape(tile_rows.shape[0], tile_rows.shape[1] // DH, DH).astype(jnp.float32)


def rounded(values_in):
    return lax.optimization_barrier(values_in.astype(jnp.bfloat16)).astype(jnp.float32)


def lookup(count_table, wanted):
    matches = wanted[..., None] == jnp.arange(count_table.shape[0], dtype=jnp.int32)
    return jnp.sum(jnp.where(matches, count_table, 0), axis=-1).astype(jnp.int32)


def key_mask(block_lists, count_table):
    key_count = jnp.where(block_lists >= 0, lookup(count_table, block_lists), 0)
    positions = jnp.arange(BQ, dtype=jnp.int32)
    return (positions[None, None, :] < key_count[..., None]).reshape(block_lists.shape[0], -1)


def scores(query_block, key_block, usable_block):
    raw_scores = jnp.einsum("qhd,khd->hqk", split_heads(query_block), split_heads(key_block))
    return jnp.where(usable_block[None, None, :], raw_scores * (DH ** -0.5), NEGATIVE)


def attend(query_block, key_block, value_block, usable_block, rows_ok):
    logits = scores(query_block, key_block, usable_block)
    highest = jnp.max(logits, axis=-1, keepdims=True)
    log_total = highest[..., 0] + jnp.log(jnp.sum(jnp.exp(logits - highest), axis=-1))
    probability = rounded(jnp.exp(logits - log_total[..., None]))
    mixture = jnp.einsum("hqk,khd->qhd", probability, split_heads(value_block))
    mixture = jnp.where(rows_ok[:, None, None], mixture, 0.0)
    return mixture.reshape(query_block.shape).astype(jnp.bfloat16), log_total


def key_terms(query_block, key_block, value_block, grad_block, log_block, delta_block, usable_block):
    probability = jnp.exp(scores(query_block, key_block, usable_block) - log_block[..., None])
    prob_grad = jnp.einsum("qhd,khd->hqk", split_heads(grad_block), split_heads(value_block))
    score_grad = rounded(probability * (prob_grad - delta_block[..., None]))
    key_part = jnp.einsum("hqk,qhd->khd", score_grad, split_heads(query_block)) * (DH ** -0.5)
    value_part = jnp.einsum("hqk,qhd->khd", rounded(probability), split_heads(grad_block))
    return score_grad, key_part.reshape(key_block.shape), value_part.reshape(key_block.shape)


def reference(query_rows, key_rows, value_rows, cotangent, neighbours, valid_counts):
    total_blocks = query_rows.shape[0]
    feature_width = query_rows.shape[2]
    positions = jnp.arange(BQ, dtype=jnp.int32)
    valid_rows = positions[None, :] < valid_counts[:, None]
    slot_index = jnp.clip(neighbours, 0, total_blocks - 1).astype(jnp.int32)
    usable = key_mask(neighbours, valid_counts)

    def forward_block(inputs):
        query_block, slot_block, usable_block, rows_ok = inputs
        key_block = key_rows[slot_block].reshape(-1, feature_width)
        value_block = value_rows[slot_block].reshape(-1, feature_width)
        return attend(query_block, key_block, value_block, usable_block, rows_ok)

    attended, log_total = lax.map(forward_block, (query_rows, slot_index, usable, valid_rows))
    grad_masked = jnp.where(valid_rows[:, :, None], cotangent, jnp.zeros_like(cotangent))
    heads_here = feature_width // DH
    attended_kept = lax.optimization_barrier(attended).astype(jnp.float32)
    row_delta = jnp.einsum("bqhd,bqhd->bhq", grad_masked.astype(jnp.float32).reshape(total_blocks, BQ, heads_here, DH), attended_kept.reshape(total_blocks, BQ, heads_here, DH))

    def backward_block(running, inputs):
        key_sum, value_sum = running
        query_block, grad_block, log_block, delta_block, slot_block, usable_block = inputs
        key_block = key_rows[slot_block].reshape(-1, feature_width)
        value_block = value_rows[slot_block].reshape(-1, feature_width)
        score_grad, key_part, value_part = key_terms(query_block, key_block, value_block, grad_block, log_block, delta_block, usable_block)
        query_part = jnp.einsum("hqk,khd->qhd", score_grad, split_heads(key_block)) * (DH ** -0.5)
        key_sum = key_sum.at[slot_block].add(key_part.reshape(-1, BQ, feature_width))
        value_sum = value_sum.at[slot_block].add(value_part.reshape(-1, BQ, feature_width))
        return (key_sum, value_sum), query_part.reshape(query_block.shape).astype(jnp.bfloat16)

    zeros_full = jnp.zeros((total_blocks, BQ, feature_width), jnp.float32)
    (key_sum, value_sum), query_grad = lax.scan(backward_block, (zeros_full, zeros_full), (query_rows, grad_masked, log_total, row_delta, slot_index, usable))
    return attended, query_grad, key_sum.astype(jnp.bfloat16), value_sum.astype(jnp.bfloat16)
```

```python
import jax
import jax.numpy as jnp
from jax import lax
from jax.experimental import pallas as pl
from jax.experimental.pallas import tpu as pltpu
from jax.sharding import PartitionSpec as P

DH = 128
BQ = 128
NEGATIVE = -1e30
SCALE = DH ** (-0.5)
RING = ("ctx", "sub")


def from_behind(array, by):
    devices = lax.axis_size(RING)
    pairs = [(i, i + by) for i in range(devices) if 0 <= i + by < devices]
    return lax.ppermute(array, RING, pairs)


def lookup(count_table, wanted):
    matches = wanted[..., None] == jnp.arange(count_table.shape[0], dtype=jnp.int32)
    return jnp.sum(jnp.where(matches, count_table, 0), axis=-1)


def mm(a, b, contract):
    return lax.dot_general(a, b, (contract, ((), ())), preferred_element_type=jnp.float32)


def attention_kernel(
    slot_ref, count_ref, valid_ref,
    qg_ref, left_ref, own_ref, right_ref,
    aq_ref, dleft_ref, down_ref, dright_ref,
    rows, cols, sums,
):
    parts, _, blocks, _, _ = own_ref.shape
    block = pl.program_id(1)
    slots = slot_ref.shape[1]

    @pl.when(block == 0)
    def _():
        for which in range(2):
            for side, ref in enumerate((left_ref, own_ref, right_ref)):
                def fill(i, carry, which=which, side=side, ref=ref):
                    tile = ref[:, which, i].reshape(BQ, DH)
                    rows[which, side * blocks + i] = tile
                    cols[which, side * blocks + i] = tile.astype(jnp.float32).T.astype(tile.dtype)
                    return carry
                lax.fori_loop(0, blocks, fill, 0)
        sums[...] = jnp.zeros_like(sums)

    index = [slot_ref[block, s] for s in range(slots)]
    gather = lambda ref, which, axis: jnp.concatenate([ref[which, i] for i in index], axis=axis)
    query = qg_ref[:, 0, 0].reshape(BQ, DH)
    grad = qg_ref[:, 1, 0].reshape(BQ, DH).astype(jnp.float32)
    valid = valid_ref[block]
    grad32 = jnp.where(lax.broadcasted_iota(jnp.int32, (BQ, DH), 0) < valid, grad, 0.0)
    grad_masked = grad32.astype(jnp.bfloat16)

    raw = mm(gather(rows, 0, 0), query, ((1,), (1,)))
    position = lax.broadcasted_iota(jnp.int32, (BQ, BQ), 0)
    logits = jnp.concatenate(
        [
            jnp.where(position < count_ref[block, s], raw[s * BQ : (s + 1) * BQ] * SCALE, NEGATIVE)
            for s in range(slots)
        ],
        axis=0,
    )
    highest = jnp.max(logits, axis=0, keepdims=True)
    weight = jnp.exp(logits - highest)
    probability = weight * (1.0 / jnp.sum(weight, axis=0, keepdims=True))
    prob16 = probability.astype(jnp.bfloat16)
    mixture = mm(gather(cols, 1, 1), prob16, ((1,), (0,)))
    row_ok = lax.broadcasted_iota(jnp.int32, (DH, BQ), 1) < valid
    attended = jnp.where(row_ok, mixture, 0.0).astype(jnp.bfloat16).astype(jnp.float32)
    delta = jnp.sum(attended * grad32.T, axis=0, keepdims=True)
    prob_grad = mm(gather(rows, 1, 0), grad_masked, ((1,), (1,)))
    score_grad = (probability * (prob_grad - delta)).astype(jnp.bfloat16)
    query_grad = mm(gather(cols, 0, 1), score_grad, ((1,), (0,))) * SCALE
    aq_ref[:, 0, 0] = attended.T.astype(jnp.bfloat16).reshape(parts, BQ // parts, DH)
    aq_ref[:, 1, 0] = query_grad.T.astype(jnp.bfloat16).reshape(parts, BQ // parts, DH)
    key_part = mm(score_grad, query, ((1,), (0,)))
    value_part = mm(prob16, grad_masked, ((1,), (0,)))
    for s in range(slots):
        here = slice(s * BQ, (s + 1) * BQ)
        sums[0, index[s]] += key_part[here]
        sums[1, index[s]] += value_part[here]

    @pl.when(block == blocks - 1)
    def _():
        for which in range(2):
            factor = SCALE if which == 0 else 1.0
            for side, ref in enumerate((dleft_ref, down_ref, dright_ref)):
                def drain(i, carry, which=which, side=side, ref=ref, factor=factor):
                    tile = sums[which, side * blocks + i] * factor
                    ref[:, which, i] = tile.astype(ref.dtype).reshape(parts, BQ // parts, DH)
                    return carry
                lax.fori_loop(0, blocks, drain, 0)


def attention(slot, count, valid, qg, left, own, right):
    parts, two, blocks, short, width = own.shape
    heads = width // DH
    one = pl.BlockSpec((parts, two, 1, short, DH), lambda h, b, *_: (0, 0, b, 0, h))
    whole = pl.BlockSpec((parts, two, blocks, short, DH), lambda h, b, *_: (0, 0, 0, 0, h))
    shape = own.shape
    pairs = blocks * heads * slot.shape[1]
    return pl.pallas_call(
        attention_kernel,
        grid_spec=pltpu.PrefetchScalarGridSpec(
            num_scalar_prefetch=3,
            grid=(heads, blocks),
            in_specs=[one, whole, whole, whole],
            out_specs=[one, whole, whole, whole],
            scratch_shapes=[
                pltpu.VMEM((2, 3 * blocks, BQ, DH), jnp.bfloat16),
                pltpu.VMEM((2, 3 * blocks, DH, BQ), jnp.bfloat16),
                pltpu.VMEM((2, 3 * blocks, BQ, DH), jnp.float32),
            ],
        ),
        out_shape=[
            jax.ShapeDtypeStruct(shape, jnp.bfloat16),
            jax.ShapeDtypeStruct(shape, jnp.bfloat16),
            jax.ShapeDtypeStruct(shape, jnp.float32),
            jax.ShapeDtypeStruct(shape, jnp.bfloat16),
        ],
        compiler_params=pltpu.CompilerParams(
            dimension_semantics=("arbitrary", "arbitrary"), vmem_limit_bytes=48 * 1024 * 1024
        ),
        cost_estimate=pl.CostEstimate(
            flops=12 * pairs * BQ * BQ * DH,
            bytes_accessed=12 * own.size * 2,
            transcendentals=pairs * BQ * BQ,
        ),
    )(slot, count, valid, qg, left, own, right)


def to_heads(first, second):
    parts = lax.axis_size("head")
    pair = jnp.stack([first, second])
    two, blocks, short, features = pair.shape
    pair = pair.reshape(two, blocks, short, parts, features // parts).transpose(3, 0, 1, 2, 4)
    return lax.all_to_all(pair, "head", split_axis=0, concat_axis=0, tiled=True)


def to_points(pair):
    pair = lax.all_to_all(pair, "head", split_axis=0, concat_axis=0, tiled=True)
    parts, two, blocks, short, width = pair.shape
    pair = pair.transpose(1, 2, 3, 0, 4).reshape(two, blocks, short, parts * width)
    return pair[0], pair[1]


def shards(query_rows, key_rows, value_rows, cotangent, neighbours, valid_counts):
    blocks = query_rows.shape[0]
    own = to_heads(key_rows, value_rows)
    left = from_behind(own, 1)
    right = from_behind(own, -1)
    qg = to_heads(query_rows, cotangent)
    first_block = lax.axis_index(RING) * blocks
    own_lists = lax.dynamic_slice_in_dim(neighbours, first_block, blocks, 0)
    own_counts = lax.dynamic_slice_in_dim(valid_counts, first_block, blocks, 0)
    slot = jnp.clip(own_lists - (first_block - blocks), 0, 3 * blocks - 1)
    count = jnp.where(own_lists >= 0, lookup(valid_counts, own_lists), 0)
    aq, dleft, down, dright = attention(slot, count, own_counts, qg, left, own, right)
    from_right = from_behind(dleft, -1).astype(jnp.float32)
    from_left = from_behind(dright, 1).astype(jnp.float32)
    attended, query_grad = to_points(aq)
    total = (down + from_right + from_left).astype(jnp.bfloat16)
    key_grad, value_grad = to_points(total)
    return (attended, query_grad, key_grad, value_grad)


def solution(mesh):
    placed = P(("groups", "ctx", "sub"), "head", None)
    return jax.shard_map(
        shards,
        mesh=mesh,
        in_specs=(placed,) * 4 + (P("groups", None), P("groups")),
        out_specs=(placed,) * 4,
        check_vma=False,
    )
```
